32 devices in a mesh: inter: 2 (over x), intra: 4 (over z), tensor: 4 (over y, core).
Axes of the slice: x: 2, y: 2, z: 4, core: 2. Of those that a mesh axis runs over, the one named last changes fastest.
Arguments:
- layer_input: bfloat16 [2048, 8192], P(('inter', 'intra')), may hold values from -6 to 6
- value_grads: bfloat16 [2048, 1024], P(('inter', 'intra'), 'tensor'), may hold values from -6 to 6
- value_weight: bfloat16 [8192, 1024], P(None, 'tensor'), may hold values from -0.0625 to 0.0625
Outputs:
- input_grads: bfloat16 [2048, 8192], P(('inter', 'intra'), 'tensor')
- weight_grads: float32 [8192, 1024], P(('inter', 'intra'), 'tensor')
The draws below stay inside these ranges and needn't reach their ends.
All inputs are finite; a program needn't handle non-finite values.
Results may differ from the reference program's by a relative error of at most 0.012.
Values may be sent and summed in bfloat16 or wider, within the bound.
A program may use at most 128 MiB of HBM per device.

```python
import jax
import jax.numpy as jnp
from jax import lax

D = 8192
KVH = 8
HD = 128
TOK_DEV = 256
NODES = 2
PER_NODE = 4
GROUPS = 8
TOKENS = 2048


def spiked(values, stream_key, source, target, parts, factor):
    owner, partner = [(jnp.arange(values.shape[dim]) // (values.shape[dim] // parts)).reshape([-1 if axis == dim else 1 for axis in range(values.ndim)]) for dim in (source, target)]
    chosen = jax.random.permutation(stream_key, parts)[partner]
    strong = (owner == chosen) | (owner == (partner + parts // 2) % parts)
    return jnp.where(strong, factor * values, values)


def block_levels(stream_key, extent, cuts, low, high):
    level, own = 1.0, jax.random.fold_in(stream_key, 6)
    for dim, shards_of in cuts:
        draws = jnp.exp(jax.random.uniform(jax.random.fold_in(own, dim), (shards_of,), jnp.float32, low / len(cuts), high / len(cuts)))
        level = level * jnp.repeat(draws, extent[dim] // shards_of).reshape([-1 if axis == dim else 1 for axis in range(len(extent))])
    return level


def noise(own_key, dims, spread, limit, cuts=(), kind=jnp.bfloat16):
    drawn = spread * jax.random.normal(own_key, dims, jnp.float32)
    if cuts:
        drawn = drawn * block_levels(own_key, dims, cuts, -0.22, 0.18)
    return jnp.clip(drawn, -limit, limit).astype(kind)


def noise_with(stream_key, dims, width, most, cuts, heavy, kind=jnp.bfloat16):
    array = width * jax.random.normal(stream_key, dims, jnp.float32)
    if cuts:
        array = array * block_levels(stream_key, dims, cuts, -0.22, 0.18)
    return jnp.clip(spiked(array, jax.random.fold_in(stream_key, 3), *heavy), -most, most).astype(kind)


def setup_inputs(seed: int = 0) -> dict:
    keys = jax.random.split(jax.random.key(seed), 4)
    layer_input = noise_with(keys[0], (TOKENS, D), 1.0, 6.0, ((0, 8),), (0, 1, 8, 2.0))
    value_grads = noise(keys[1], (TOKENS, KVH * HD), 1.0, 6.0, ((0, 8), (1, 4)))
    value_weight = noise(keys[2], (D, KVH * HD), D ** -0.5, 0.0625, ((1, 4),))
    return dict(layer_input=layer_input, value_grads=value_grads, value_weight=value_weight)


def block_scale(values):
    largest = jnp.max(jnp.abs(values), axis=-1)
    scale = (largest / 7.0 + 1e-6).astype(jnp.bfloat16)
    levels = (values / scale.astype(values.dtype)[..., None]).astype(jnp.bfloat16)
    return levels, scale


def restore(levels, scale):
    return levels.astype(jnp.float32) * scale.astype(jnp.float32)[..., None]


def reference(layer_input, value_grads, value_weight):
    weight_heads = value_weight.astype(jnp.float32).reshape(D, KVH, HD)

    def group_input_grads(grads):
        heads_view = grads.astype(jnp.float32).reshape(TOK_DEV, KVH, HD)
        terms = jnp.einsum("thk,fhk->htf", heads_view, weight_heads)
        terms = lax.optimization_barrier(terms.astype(jnp.bfloat16))
        return jnp.sum(terms.astype(jnp.float32), axis=0).astype(jnp.bfloat16)

    grouped_grads = value_grads.reshape(GROUPS, TOK_DEV, KVH * HD)
    input_grads = lax.map(group_input_grads, grouped_grads).reshape(TOKENS, D)

    inputs_nodes = layer_input.reshape(NODES, PER_NODE, TOK_DEV, D)
    grads_nodes = value_grads.reshape(NODES, PER_NODE, TOK_DEV, KVH * HD)

    def node_total(pair):
        node_inputs, node_grads = pair

        def add_group(total, group):
            rows_in, rows_grad = group
            partial_value = jnp.dot(rows_in.T, rows_grad, preferred_element_type=jnp.float32)
            levels, scale = block_scale(partial_value.reshape(D, KVH, HD))
            return total + restore(levels, scale), None

        start = jnp.zeros((D, KVH, HD), jnp.float32)
        total, unused = lax.scan(add_group, start, (node_inputs, node_grads))
        return total

    node_sum = lax.map(node_total, (inputs_nodes, grads_nodes))
    levels, scale = block_scale(node_sum)
    weight_grads = jnp.sum(restore(levels, scale), axis=0) / float(GROUPS)
    return input_grads, weight_grads.reshape(D, KVH * HD)
```

```python
import functools

import jax
import jax.numpy as jnp
from jax import lax
from jax.experimental import pallas as pl
from jax.experimental.pallas import tpu as pltpu
from jax.sharding import PartitionSpec as P

HD = 128
MESH = pl.DeviceIdType.MESH
DIRECT = 0
TERM_CHUNKS = 4
TILE = 256
ORDER = (2, 3, 6, 7, 1, 5, 4)


def block_scale(values):
    largest = jnp.max(jnp.abs(values), axis=-1)
    scale = (largest / 7.0 + 1e-06).astype(jnp.bfloat16)
    levels = (values / scale.astype(values.dtype)[..., None]).astype(jnp.bfloat16)
    return (levels, scale)


def restore(levels, scale):
    return levels.astype(jnp.float32) * scale.astype(jnp.float32)[..., None]


def plain_body(layer_input, value_grads, value_weight):
    tok_rows = layer_input.shape[0]
    width = layer_input.shape[1]
    heads_here = value_grads.shape[1] // HD
    grads_view = value_grads.reshape(tok_rows, heads_here, HD)
    weight_view = value_weight.reshape(width, heads_here, HD)
    terms = jnp.einsum("thk,fhk->htf", grads_view, weight_view, preferred_element_type=jnp.float32)
    shares = lax.psum_scatter(
        terms.astype(jnp.bfloat16), "tensor", scatter_dimension=2, tiled=True
    ).astype(jnp.float32)
    input_grads = jnp.sum(shares, axis=0).astype(jnp.bfloat16)
    partial_value = jnp.einsum(
        "td,tc->dc", layer_input, value_grads, preferred_element_type=jnp.float32
    )
    nodes = lax.axis_size("inter")
    inner = lax.axis_size("intra")
    segment = width // (nodes * inner)
    levels, scale = block_scale(partial_value.reshape(width, heads_here, HD))
    levels = levels.reshape(nodes, inner, segment, heads_here, HD)
    scale = scale.reshape(nodes, inner, segment, heads_here)
    got_levels, got_scale = (
        lax.all_to_all(levels, "intra", split_axis=1, concat_axis=1, tiled=True),
        lax.all_to_all(scale, "intra", split_axis=1, concat_axis=1, tiled=True),
    )
    node_sum = jnp.sum(restore(got_levels, got_scale), axis=1)
    second_levels, second_scale = block_scale(node_sum)
    far_levels, far_scale = (
        lax.all_to_all(second_levels, "inter", split_axis=0, concat_axis=0, tiled=True),
        lax.all_to_all(second_scale, "inter", split_axis=0, concat_axis=0, tiled=True),
    )
    total = jnp.sum(restore(far_levels, far_scale), axis=0) / float(nodes * inner)
    weight_grads = total.reshape(segment, heads_here * HD)
    return (input_grads, weight_grads)


def quantized(values):
    view = values.reshape(values.shape[0] // HD, HD, values.shape[1])
    largest = jnp.max(jnp.abs(view), axis=1, keepdims=True)
    scale = (largest / 7.0 + 1e-6).astype(jnp.bfloat16).astype(jnp.float32)
    levels = (view * (1.0 / scale)).astype(jnp.bfloat16).astype(jnp.float32)
    return (levels * scale).reshape(values.shape)


def kernel(
    li, vg, w, ig, wg,
    parts, grads, mate_grads, weights, outgoing, incoming, own_terms, sums,
    li_send, li_recv, vg_send, vg_recv, w_send, w_recv, term_send, term_recv, local,
):
    tok, width = li.shape
    segment = width // 8
    block = width // 4
    rows_chunk = block // TERM_CHUNKS
    quarter = (tok - DIRECT) // 4
    i, j, t = lax.axis_index("inter"), lax.axis_index("intra"), lax.axis_index("tensor")
    y, c = t // 2, t % 2
    t_core, t_y = t + 1 - 2 * c, (t + 2) % 4
    along = (j, j + 1 - 2 * (j % 2), (j + 2) % 4, 3 - j)
    inner = j % 3 != 0

    def place(k):
        return (i if k < 4 else 1 - i), along[k % 4]

    def device(k):
        return (*place(k), t)

    mate, across = (i, j, t_core), (i, j, t_y)

    def columns(k):
        ip, jp = place(k)
        return pl.ds(pl.multiple_of((ip * 4 + jp) * segment, segment), segment)

    direct_rows = pl.ds(pl.multiple_of(c * (DIRECT // 2), 16), DIRECT // 2)
    my_rows = pl.ds(pl.multiple_of(DIRECT + t * quarter, 16), quarter)
    y_rows = pl.ds(pl.multiple_of(DIRECT + t_y * quarter, 16), quarter)

    def remote(src, dst, send, recv, where):
        return pltpu.make_async_remote_copy(
            src_ref=src, dst_ref=dst, send_sem=send, recv_sem=recv,
            device_id=where, device_id_type=MESH,
        )

    def weight_rows(b, core, chunk, count):
        owner = (1 - y if b == 0 else y) * 2 + core
        return pl.ds(pl.multiple_of(owner * block + chunk * rows_chunk, rows_chunk), count * rows_chunk)

    weight_pieces = [(0, n, 1) for n in range(TERM_CHUNKS)] + [(1, 0, TERM_CHUNKS)]
    held = [
        pltpu.make_async_copy(
            w.at[weight_rows(b, c, n, count), :],
            weights.at[0, b, pl.ds(n * rows_chunk, count * rows_chunk), :],
            local.at[index],
        )
        for index, (b, n, count) in enumerate(weight_pieces)
    ]
    own_part = pltpu.make_async_copy(li.at[:, columns(0)], parts.at[0], local.at[len(held)])
    for copy in held:
        copy.start()
    own_part.start()

    barrier = pltpu.get_barrier_semaphore()
    friends = [device(k) for k in range(1, 8)] + [mate, across]
    for friend in friends:
        pl.semaphore_signal(barrier, inc=1, device_id=friend, device_id_type=MESH)
    pl.semaphore_wait(barrier, len(friends))

    sent = []

    def start(copy):
        copy.start()
        sent.append(copy)
        return copy

    mate_copy = start(remote(vg, mate_grads, vg_send.at[9], vg_recv.at[0], mate))

    def grads_hop(index, src, slot, where):
        return remote(src, grads.at[slot], vg_send.at[index], vg_recv.at[slot], where)

    start(grads_hop(0, vg, 1, device(1)))
    inner_hops = [
        grads_hop(1, vg, 3, device(3)),
        grads_hop(2, grads.at[1], 2, device(3)),
        grads_hop(3, grads.at[3], 2, device(1)),
        grads_hop(4, grads.at[2], 3, device(1)),
    ]

    @pl.when(inner)
    def _():
        inner_hops[0].start()

    x_hops = [grads_hop(5 + s, vg if s == 0 else grads.at[s], 4 + s, device(4)) for s in range(4)]
    start(x_hops[0])

    swaps = [
        start(remote(
            w.at[weight_rows(b, 1 - c, n, count), :],
            weights.at[1, b, pl.ds(n * rows_chunk, count * rows_chunk), :],
            w_send.at[index], w_recv.at[index], mate,
        ))
        for index, (b, n, count) in enumerate(weight_pieces)
    ]

    def li_hop(kind, k, src, rows, where):
        return remote(src, parts.at[k, rows, :], li_send.at[kind, k], li_recv.at[kind, k], where)

    direct, shared, to_y, core_direct, core_shared, core_y = ({} for _ in range(6))
    for k in ORDER:
        if DIRECT:
            direct[k] = start(li_hop(0, k, li.at[direct_rows, columns(k)], direct_rows, device(k)))
            core_direct[k] = li_hop(3, k, parts.at[k, direct_rows, :], direct_rows, mate)
        shared[k] = start(li_hop(1, k, li.at[my_rows, columns(k)], my_rows, device(k)))
        to_y[k] = li_hop(2, k, parts.at[k, my_rows, :], my_rows, across)
        core_shared[k] = li_hop(4, k, parts.at[k, my_rows, :], my_rows, mate)
        core_y[k] = li_hop(5, k, parts.at[k, y_rows, :], y_rows, mate)

    def product(b, rows):
        dims = (((1,), (1,)), ((), ()))
        return lax.dot_general(
            vg[...], weights[0, b, rows, :], dims, preferred_element_type=jnp.float32
        ) + lax.dot_general(
            mate_grads[...], weights[1, b, rows, :], dims, preferred_element_type=jnp.float32
        )

    terms = [
        remote(outgoing.at[n], incoming.at[n], term_send.at[n], term_recv.at[n], across)
        for n in range(TERM_CHUNKS)
    ]

    def send_term(n):
        held[n].wait()
        swaps[n].wait_recv()

        @pl.loop(0, rows_chunk // TILE)
        def _(s):
            at = pl.multiple_of(s * TILE, TILE)
            outgoing[n, :, pl.ds(at, TILE)] = product(
                0, pl.ds(n * rows_chunk + at, TILE)
            ).astype(jnp.bfloat16)

        start(terms[n])

    def got_grads(slot):
        grads_hop(0, vg, slot, device(1)).wait_recv()

    def add_partial(k, first):
        side = k // 4

        @pl.loop(0, segment // TILE)
        def _(s):
            at = pl.ds(pl.multiple_of(s * TILE, TILE), TILE)
            value = lax.dot_general(
                (vg if k == 0 else grads.at[k])[...], parts[k, :, at],
                (((0,), (0,)), ((), ())), preferred_element_type=jnp.float32,
            )
            value = quantized(value)
            sums[side, :, at] = value if first else sums[side, :, at] + value

    mate_copy.wait_recv()
    send_term(0)
    got_grads(1)

    @pl.when(inner)
    def _():
        inner_hops[1].start()

    start(x_hops[1])
    send_term(1)
    got_grads(3)

    @pl.when(inner)
    def _():
        inner_hops[2].start()

    start(x_hops[3])
    send_term(2)
    got_grads(2)

    @pl.when(inner)
    def _():
        inner_hops[3].start()

    start(x_hops[2])
    send_term(3)

    own_part.wait()
    add_partial(0, True)

    def keep_own_terms():
        held[TERM_CHUNKS].wait()
        swaps[TERM_CHUNKS].wait_recv()

        @pl.loop(0, block // TILE)
        def _(s):
            at = pl.ds(pl.multiple_of(s * TILE, TILE), TILE)
            own_terms[:, at] = product(1, at)

    def finish_terms():
        for n in range(TERM_CHUNKS):
            terms[n].wait_recv()
            at = pl.ds(n * rows_chunk, rows_chunk)
            ig[:, at] = (own_terms[:, at] + incoming[n].astype(jnp.float32)).astype(jnp.bfloat16)

    started = {0}
    for step in range(len(ORDER) + 2):
        if step < len(ORDER):
            k = ORDER[step]
            if DIRECT:
                direct[k].wait_recv()
                start(core_direct[k])
            shared[k].wait_recv()
            start(to_y[k])
            start(core_shared[k])
        if 1 <= step <= len(ORDER):
            k = ORDER[step - 1]
            to_y[k].wait_recv()
            start(core_y[k])
        if step == 1:
            keep_own_terms()
        if step == len(ORDER):
            finish_terms()
        if step >= 2:
            k = ORDER[step - 2]
            if DIRECT:
                core_direct[k].wait_recv()
            core_shared[k].wait_recv()
            core_y[k].wait_recv()
            if k >= 4:
                got_grads(k)
            add_partial(k, k // 4 not in started)
            started.add(k // 4)

    @pl.loop(0, segment // TILE)
    def _(s):
        at = pl.ds(pl.multiple_of(s * TILE, TILE), TILE)
        wg[:, at] = (quantized(sums[0, :, at]) + quantized(sums[1, :, at])) * 0.125

    for copy in sent:
        copy.wait_send()

    @pl.when(inner)
    def _():
        for copy in inner_hops:
            copy.wait_send()


def kernel_body(layer_input, value_grads, value_weight):
    tok, width = layer_input.shape
    cols = value_grads.shape[1]
    segment, block = width // 8, width // 4
    bf16, f32 = jnp.bfloat16, jnp.float32
    dma = pltpu.SemaphoreType.DMA
    in_vmem, in_any = pl.BlockSpec(memory_space=pltpu.VMEM), pl.BlockSpec(memory_space=pl.ANY)
    input_grads, weight_grads = pl.pallas_call(
        kernel,
        out_shape=(
            jax.ShapeDtypeStruct((tok, block), bf16),
            jax.ShapeDtypeStruct((cols, segment), f32),
        ),
        in_specs=[in_any, in_vmem, in_any],
        out_specs=(in_vmem, in_vmem),
        scratch_shapes=[
            pltpu.VMEM((8, tok, segment), bf16),
            pltpu.VMEM((8, tok, cols), bf16),
            pltpu.VMEM((tok, cols), bf16),
            pltpu.VMEM((2, 2, block, cols), bf16),
            pltpu.VMEM((TERM_CHUNKS, tok, block // TERM_CHUNKS), bf16),
            pltpu.VMEM((TERM_CHUNKS, tok, block // TERM_CHUNKS), bf16),
            pltpu.VMEM((tok, block), f32),
            pltpu.VMEM((2, cols, segment), f32),
            dma((6, 8)), dma((6, 8)),
            dma((10,)), dma((8,)),
            dma((TERM_CHUNKS + 1,)), dma((TERM_CHUNKS + 1,)),
            dma((TERM_CHUNKS,)), dma((TERM_CHUNKS,)),
            dma((TERM_CHUNKS + 2,)),
        ],
        compiler_params=pltpu.CompilerParams(
            collective_id=0, has_side_effects=True, vmem_limit_bytes=48 * 1024 * 1024
        ),
        cost_estimate=pl.CostEstimate(
            flops=4 * tok * width * cols, bytes_accessed=12 * 1024 * 1024, transcendentals=0
        ),
    )(layer_input, value_grads, value_weight)
    return input_grads, weight_grads.T


def solution(mesh):
    placed = (P(("inter", "intra"), None), P(("inter", "intra"), "tensor"), P(None, "tensor"))
    sizes = tuple(mesh.shape[name] for name in ("inter", "intra", "tensor"))
    return jax.shard_map(
        kernel_body if sizes == (2, 4, 4) else plain_body,
        mesh=mesh,
        in_specs=placed,
        out_specs=(P(("inter", "intra"), "tensor"), P(("inter", "intra"), "tensor")),
        check_vma=False,
    )
```

```python
import functools

import jax
import jax.numpy as jnp
from jax import lax
from jax.experimental import pallas as pl
from jax.experimental.pallas import tpu as pltpu
from jax.sharding import PartitionSpec as P

HD = 128
MESH = pl.DeviceIdType.MESH
DIRECT = 64
TERM_CHUNKS = 4
TILE = 256
SEND_ORDER = (2, 1, 3, 4, 6, 5, 7)
WAIT_ORDER = (2, 1, 3, 4, 6, 5, 7)
WINDOW = 4


def block_scale(values):
    largest = jnp.max(jnp.abs(values), axis=-1)
    scale = (largest / 7.0 + 1e-06).astype(jnp.bfloat16)
    levels = (values / scale.astype(values.dtype)[..., None]).astype(jnp.bfloat16)
    return (levels, scale)


def restore(levels, scale):
    return levels.astype(jnp.float32) * scale.astype(jnp.float32)[..., None]


def plain_body(layer_input, value_grads, value_weight):
    tok_rows = layer_input.shape[0]
    width = layer_input.shape[1]
    heads_here = value_grads.shape[1] // HD
    grads_view = value_grads.reshape(tok_rows, heads_here, HD)
    weight_view = value_weight.reshape(width, heads_here, HD)
    terms = jnp.einsum("thk,fhk->htf", grads_view, weight_view, preferred_element_type=jnp.float32)
    shares = lax.psum_scatter(
        terms.astype(jnp.bfloat16), "tensor", scatter_dimension=2, tiled=True
    ).astype(jnp.float32)
    input_grads = jnp.sum(shares, axis=0).astype(jnp.bfloat16)
    partial_value = jnp.einsum(
        "td,tc->dc", layer_input, value_grads, preferred_element_type=jnp.float32
    )
    nodes = lax.axis_size("inter")
    inner = lax.axis_size("intra")
    segment = width // (nodes * inner)
    levels, scale = block_scale(partial_value.reshape(width, heads_here, HD))
    levels = levels.reshape(nodes, inner, segment, heads_here, HD)
    scale = scale.reshape(nodes, inner, segment, heads_here)
    got_levels, got_scale = (
        lax.all_to_all(levels, "intra", split_axis=1, concat_axis=1, tiled=True),
        lax.all_to_all(scale, "intra", split_axis=1, concat_axis=1, tiled=True),
    )
    node_sum = jnp.sum(restore(got_levels, got_scale), axis=1)
    second_levels, second_scale = block_scale(node_sum)
    far_levels, far_scale = (
        lax.all_to_all(second_levels, "inter", split_axis=0, concat_axis=0, tiled=True),
        lax.all_to_all(second_scale, "inter", split_axis=0, concat_axis=0, tiled=True),
    )
    total = jnp.sum(restore(far_levels, far_scale), axis=0) / float(nodes * inner)
    weight_grads = total.reshape(segment, heads_here * HD)
    return (input_grads, weight_grads)


def quantized(values):
    view = values.reshape(values.shape[0] // HD, HD, values.shape[1])
    largest = jnp.max(jnp.abs(view), axis=1, keepdims=True)
    scale = (largest / 7.0 + 1e-6).astype(jnp.bfloat16).astype(jnp.float32)
    levels = (view * (1.0 / scale)).astype(jnp.bfloat16).astype(jnp.float32)
    return (levels * scale).reshape(values.shape)


def kernel(
    li, vg_hbm, w, ig, wg,
    vg, parts, grads, mate_grads, weights, outgoing, incoming, own_terms, sums,
    li_send, li_recv, vg_send, vg_recv, w_send, w_recv, term_send, term_recv, local,
):
    tok, width = li.shape
    segment = width // 8
    block = width // 4
    rows_chunk = block // TERM_CHUNKS
    quarter = (tok - DIRECT) // 4
    i, j, t = lax.axis_index("inter"), lax.axis_index("intra"), lax.axis_index("tensor")
    y, c = t // 2, t % 2
    t_core, t_y = t + 1 - 2 * c, (t + 2) % 4
    along = (j, j + 1 - 2 * (j % 2), (j + 2) % 4, 3 - j)

    def place(k):
        return (i if k < 4 else 1 - i), along[k % 4]

    def device(k):
        return (*place(k), t)

    mate, across = (i, j, t_core), (i, j, t_y)

    def columns(k):
        ip, jp = place(k)
        return pl.ds(pl.multiple_of((ip * 4 + jp) * segment, segment), segment)

    direct_rows = pl.ds(pl.multiple_of(c * (DIRECT // 2), 16), DIRECT // 2)
    my_rows = pl.ds(pl.multiple_of(DIRECT + t * quarter, 16), quarter)
    y_rows = pl.ds(pl.multiple_of(DIRECT + t_y * quarter, 16), quarter)

    def remote(src, dst, send, recv, where):
        return pltpu.make_async_remote_copy(
            src_ref=src, dst_ref=dst, send_sem=send, recv_sem=recv,
            device_id=where, device_id_type=MESH,
        )

    def weight_rows(b, core, chunk, count):
        owner = (1 - y if b == 0 else y) * 2 + core
        return pl.ds(pl.multiple_of(owner * block + chunk * rows_chunk, rows_chunk), count * rows_chunk)

    weight_pieces = [(0, n, 1) for n in range(TERM_CHUNKS)] + [(1, 0, TERM_CHUNKS)]
    held = [
        pltpu.make_async_copy(
            w.at[weight_rows(b, c, n, count), :],
            weights.at[0, b, pl.ds(n * rows_chunk, count * rows_chunk), :],
            local.at[index],
        )
        for index, (b, n, count) in enumerate(weight_pieces)
    ]
    own_part = pltpu.make_async_copy(li.at[:, columns(0)], parts.at[0], local.at[len(held)])
    own_grads = pltpu.make_async_copy(vg_hbm, vg, local.at[len(held) + 1])
    own_grads.start()
    for copy in held:
        copy.start()
    own_part.start()

    barrier = pltpu.get_barrier_semaphore()
    friends = [device(k) for k in range(1, 8)] + [mate, across]
    for friend in friends:
        pl.semaphore_signal(barrier, inc=1, device_id=friend, device_id_type=MESH)
    pl.semaphore_wait(barrier, len(friends))

    sent = []

    def start(copy):
        copy.start()
        sent.append(copy)
        return copy

    mate_copy = start(remote(vg_hbm, mate_grads, vg_send.at[7], vg_recv.at[0], mate))

    def grads_hop(index, src, slot, where):
        return remote(src, grads.at[slot], vg_send.at[index], vg_recv.at[slot], where)

    start(grads_hop(0, vg_hbm, 1, device(1)))
    start(grads_hop(1, vg_hbm, 3, device(3)))
    start(grads_hop(3, vg_hbm, 4, device(4)))

    def pass_grads(slot):
        got_grads(slot)
        if slot == 3:
            start(grads_hop(2, grads.at[3], 2, device(1)))
        start(grads_hop(3 + slot, grads.at[slot], 4 + slot, device(4)))

    swaps = [
        start(remote(
            w.at[weight_rows(b, 1 - c, n, count), :],
            weights.at[1, b, pl.ds(n * rows_chunk, count * rows_chunk), :],
            w_send.at[index], w_recv.at[index], mate,
        ))
        for index, (b, n, count) in enumerate(weight_pieces)
    ]

    def li_hop(kind, k, src, rows, where):
        return remote(src, parts.at[k, rows, :], li_send.at[kind, k], li_recv.at[kind, k], where)

    direct, shared, to_y, core_direct, core_shared, core_y = ({} for _ in range(6))
    for k in SEND_ORDER:
        if DIRECT:
            direct[k] = li_hop(0, k, li.at[direct_rows, columns(k)], direct_rows, device(k))
            core_direct[k] = li_hop(3, k, parts.at[k, direct_rows, :], direct_rows, mate)
        shared[k] = li_hop(1, k, li.at[my_rows, columns(k)], my_rows, device(k))
        to_y[k] = li_hop(2, k, parts.at[k, my_rows, :], my_rows, across)
        core_shared[k] = li_hop(4, k, parts.at[k, my_rows, :], my_rows, mate)
        core_y[k] = li_hop(5, k, parts.at[k, y_rows, :], y_rows, mate)

    def send_piece(n):
        k = SEND_ORDER[n]
        if DIRECT:
            direct[k].start()
        shared[k].start()

    def sent_piece(n):
        k = SEND_ORDER[n]
        if DIRECT:
            direct[k].wait_send()
        shared[k].wait_send()

    for n in range(WINDOW):
        send_piece(n)

    def product(b, rows):
        dims = (((1,), (1,)), ((), ()))
        return lax.dot_general(
            vg[...], weights[0, b, rows, :], dims, preferred_element_type=jnp.float32
        ) + lax.dot_general(
            mate_grads[...], weights[1, b, rows, :], dims, preferred_element_type=jnp.float32
        )

    terms = [
        remote(outgoing.at[n], incoming.at[n], term_send.at[n], term_recv.at[n], across)
        for n in range(TERM_CHUNKS)
    ]

    def send_term(n):
        held[n].wait()
        swaps[n].wait_recv()

        @pl.loop(0, rows_chunk // TILE)
        def _(s):
            at = pl.multiple_of(s * TILE, TILE)
            outgoing[n, :, pl.ds(at, TILE)] = product(
                0, pl.ds(n * rows_chunk + at, TILE)
            ).astype(jnp.bfloat16)

        start(terms[n])

    def got_grads(slot):
        grads_hop(0, vg_hbm, slot, device(1)).wait_recv()

    def add_partial(k, first):
        side = k // 4

        @pl.loop(0, segment // TILE)
        def _(s):
            at = pl.ds(pl.multiple_of(s * TILE, TILE), TILE)
            value = lax.dot_general(
                (vg if k == 0 else grads.at[k])[...], parts[k, :, at],
                (((0,), (0,)), ((), ())), preferred_element_type=jnp.float32,
            )
            value = quantized(value)
            sums[side, :, at] = value if first else sums[side, :, at] + value

    own_grads.wait()
    mate_copy.wait_recv()
    for n in range(TERM_CHUNKS):
        send_term(n)
        if n == 1:
            pass_grads(1)
        if n == 3:
            pass_grads(3)

    own_part.wait()
    add_partial(0, True)

    def keep_own_terms():
        held[TERM_CHUNKS].wait()
        swaps[TERM_CHUNKS].wait_recv()

        @pl.loop(0, block // TILE)
        def _(s):
            at = pl.ds(pl.multiple_of(s * TILE, TILE), TILE)
            own_terms[:, at] = product(1, at)

    def finish_terms():
        for n in range(TERM_CHUNKS):
            terms[n].wait_recv()
            at = pl.ds(n * rows_chunk, rows_chunk)
            ig[:, at] = (own_terms[:, at] + incoming[n].astype(jnp.float32)).astype(jnp.bfloat16)

    started = {0}
    for step in range(len(WAIT_ORDER) + 2):
        if step < len(WAIT_ORDER):
            k = WAIT_ORDER[step]
            if DIRECT:
                direct[k].wait_recv()
                start(core_direct[k])
            shared[k].wait_recv()
            start(to_y[k])
            start(core_shared[k])
            sent_piece(step)
            if step + WINDOW < len(SEND_ORDER):
                send_piece(step + WINDOW)
        if 1 <= step <= len(WAIT_ORDER):
            k = WAIT_ORDER[step - 1]
            to_y[k].wait_recv()
            start(core_y[k])
        if step == 2:
            pass_grads(2)
        if step == 1:
            keep_own_terms()
        if step == len(WAIT_ORDER):
            finish_terms()
        if step >= 2:
            k = WAIT_ORDER[step - 2]
            if DIRECT:
                core_direct[k].wait_recv()
            core_shared[k].wait_recv()
            core_y[k].wait_recv()
            if k >= 4:
                got_grads(k)
            add_partial(k, k // 4 not in started)
            started.add(k // 4)

    @pl.loop(0, segment // TILE)
    def _(s):
        at = pl.ds(pl.multiple_of(s * TILE, TILE), TILE)
        wg[:, at] = (quantized(sums[0, :, at]) + quantized(sums[1, :, at])) * 0.125

    for copy in sent:
        copy.wait_send()


def kernel_body(layer_input, value_grads, value_weight):
    tok, width = layer_input.shape
    cols = value_grads.shape[1]
    segment, block = width // 8, width // 4
    bf16, f32 = jnp.bfloat16, jnp.float32
    dma = pltpu.SemaphoreType.DMA
    in_vmem, in_any = pl.BlockSpec(memory_space=pltpu.VMEM), pl.BlockSpec(memory_space=pl.ANY)
    input_grads, weight_grads = pl.pallas_call(
        kernel,
        out_shape=(
            jax.ShapeDtypeStruct((tok, block), bf16),
            jax.ShapeDtypeStruct((cols, segment), f32),
        ),
        in_specs=[in_any, in_any, in_any],
        out_specs=(in_vmem, in_vmem),
        scratch_shapes=[
            pltpu.VMEM((tok, cols), bf16),
            pltpu.VMEM((8, tok, segment), bf16),
            pltpu.VMEM((8, tok, cols), bf16),
            pltpu.VMEM((tok, cols), bf16),
            pltpu.VMEM((2, 2, block, cols), bf16),
            pltpu.VMEM((TERM_CHUNKS, tok, block // TERM_CHUNKS), bf16),
            pltpu.VMEM((TERM_CHUNKS, tok, block // TERM_CHUNKS), bf16),
            pltpu.VMEM((tok, block), f32),
            pltpu.VMEM((2, cols, segment), f32),
            dma((6, 8)), dma((6, 8)),
            dma((8,)), dma((8,)),
            dma((TERM_CHUNKS + 1,)), dma((TERM_CHUNKS + 1,)),
            dma((TERM_CHUNKS,)), dma((TERM_CHUNKS,)),
            dma((TERM_CHUNKS + 3,)),
        ],
        compiler_params=pltpu.CompilerParams(
            collective_id=0, has_side_effects=True, vmem_limit_bytes=48 * 1024 * 1024
        ),
        cost_estimate=pl.CostEstimate(
            flops=4 * tok * width * cols, bytes_accessed=12 * 1024 * 1024, transcendentals=0
        ),
    )(layer_input, value_grads, value_weight)
    return input_grads, weight_grads.T


def solution(mesh):
    placed = (P(("inter", "intra"), None), P(("inter", "intra"), "tensor"), P(None, "tensor"))
    sizes = tuple(mesh.shape[name] for name in ("inter", "intra", "tensor"))
    return jax.shard_map(
        kernel_body if sizes == (2, 4, 4) else plain_body,
        mesh=mesh,
        in_specs=placed,
        out_specs=(P(("inter", "intra"), "tensor"), P(("inter", "intra"), "tensor")),
        check_vma=False,
    )
```

```python
import functools

import jax
import jax.numpy as jnp
from jax import lax
from jax.experimental import pallas as pl
from jax.experimental.pallas import tpu as pltpu
from jax.sharding import PartitionSpec as P

HD = 128
MESH = pl.DeviceIdType.MESH
DIRECT = 64
TERM_CHUNKS = 4
TERM_TILE = 512
TILE = 1024
SEND_ORDER = (2, 1, 3, 4, 6, 5, 7)
WAIT_ORDER = (2, 1, 3, 4, 6, 5, 7)
WINDOW = 4


def block_scale(values):
    largest = jnp.max(jnp.abs(values), axis=-1)
    scale = (largest / 7.0 + 1e-06).astype(jnp.bfloat16)
    levels = (values / scale.astype(values.dtype)[..., None]).astype(jnp.bfloat16)
    return (levels, scale)


def restore(levels, scale):
    return levels.astype(jnp.float32) * scale.astype(jnp.float32)[..., None]


def plain_body(layer_input, value_grads, value_weight):
    tok_rows = layer_input.shape[0]
    width = layer_input.shape[1]
    heads_here = value_grads.shape[1] // HD
    grads_view = value_grads.reshape(tok_rows, heads_here, HD)
    weight_view = value_weight.reshape(width, heads_here, HD)
    terms = jnp.einsum("thk,fhk->htf", grads_view, weight_view, preferred_element_type=jnp.float32)
    shares = lax.psum_scatter(
        terms.astype(jnp.bfloat16), "tensor", scatter_dimension=2, tiled=True
    ).astype(jnp.float32)
    input_grads = jnp.sum(shares, axis=0).astype(jnp.bfloat16)
    partial_value = jnp.einsum(
        "td,tc->dc", layer_input, value_grads, preferred_element_type=jnp.float32
    )
    nodes = lax.axis_size("inter")
    inner = lax.axis_size("intra")
    segment = width // (nodes * inner)
    levels, scale = block_scale(partial_value.reshape(width, heads_here, HD))
    levels = levels.reshape(nodes, inner, segment, heads_here, HD)
    scale = scale.reshape(nodes, inner, segment, heads_here)
    got_levels, got_scale = (
        lax.all_to_all(levels, "intra", split_axis=1, concat_axis=1, tiled=True),
        lax.all_to_all(scale, "intra", split_axis=1, concat_axis=1, tiled=True),
    )
    node_sum = jnp.sum(restore(got_levels, got_scale), axis=1)
    second_levels, second_scale = block_scale(node_sum)
    far_levels, far_scale = (
        lax.all_to_all(second_levels, "inter", split_axis=0, concat_axis=0, tiled=True),
        lax.all_to_all(second_scale, "inter", split_axis=0, concat_axis=0, tiled=True),
    )
    total = jnp.sum(restore(far_levels, far_scale), axis=0) / float(nodes * inner)
    weight_grads = total.reshape(segment, heads_here * HD)
    return (input_grads, weight_grads)


def quantized(values):
    view = values.reshape(values.shape[0] // HD, HD, values.shape[1])
    largest = jnp.max(jnp.abs(view), axis=1, keepdims=True)
    scale = (largest / 7.0 + 1e-6).astype(jnp.bfloat16).astype(jnp.float32)
    levels = (view * (1.0 / scale)).astype(jnp.bfloat16).astype(jnp.float32)
    return (levels * scale).reshape(values.shape)


def kernel(
    li, vg_hbm, w, ig, wg,
    pair, flipped, parts, grads, weights, outgoing, incoming, own_terms, sums,
    li_send, li_recv, vg_send, vg_recv, w_send, w_recv, term_send, term_recv, local,
):
    tok, width = li.shape
    segment = width // 8
    block = width // 4
    rows_chunk = block // TERM_CHUNKS
    quarter = (tok - DIRECT) // 4
    cols = vg_hbm.shape[1]
    mine, other = pl.ds(0, cols), pl.ds(cols, cols)
    i, j, t = lax.axis_index("inter"), lax.axis_index("intra"), lax.axis_index("tensor")
    y, c = t // 2, t % 2
    t_core, t_y = t + 1 - 2 * c, (t + 2) % 4
    along = (j, j + 1 - 2 * (j % 2), (j + 2) % 4, 3 - j)

    def place(k):
        return (i if k < 4 else 1 - i), along[k % 4]

    def device(k):
        return (*place(k), t)

    mate, across = (i, j, t_core), (i, j, t_y)

    def columns(k):
        ip, jp = place(k)
        return pl.ds(pl.multiple_of((ip * 4 + jp) * segment, segment), segment)

    direct_rows = pl.ds(pl.multiple_of(c * (DIRECT // 2), 16), DIRECT // 2)
    my_rows = pl.ds(pl.multiple_of(DIRECT + t * quarter, 16), quarter)
    y_rows = pl.ds(pl.multiple_of(DIRECT + t_y * quarter, 16), quarter)

    def remote(src, dst, send, recv, where):
        return pltpu.make_async_remote_copy(
            src_ref=src, dst_ref=dst, send_sem=send, recv_sem=recv,
            device_id=where, device_id_type=MESH,
        )

    def weight_rows(b, core, chunk, count):
        owner = (1 - y if b == 0 else y) * 2 + core
        return pl.ds(pl.multiple_of(owner * block + chunk * rows_chunk, rows_chunk), count * rows_chunk)

    weight_pieces = [(0, n, 1) for n in range(TERM_CHUNKS)] + [(1, 0, TERM_CHUNKS)]
    held = [
        pltpu.make_async_copy(
            w.at[weight_rows(b, c, n, count), :],
            weights.at[b, pl.ds(n * rows_chunk, count * rows_chunk), mine],
            local.at[index],
        )
        for index, (b, n, count) in enumerate(weight_pieces)
    ]
    own_part = pltpu.make_async_copy(li.at[:, columns(0)], parts.at[0], local.at[len(held)])
    own_grads = pltpu.make_async_copy(vg_hbm, pair.at[:, mine], local.at[len(held) + 1])
    own_grads.start()
    for copy in held:
        copy.start()
    own_part.start()
    own_grads.wait()
    flipped[...] = pair[:, mine].T

    barrier = pltpu.get_barrier_semaphore()
    friends = [device(k) for k in range(1, 8)] + [mate, across]
    for friend in friends:
        pl.semaphore_signal(barrier, inc=1, device_id=friend, device_id_type=MESH)
    pl.semaphore_wait(barrier, len(friends))

    sent = []

    def start(copy):
        copy.start()
        sent.append(copy)
        return copy

    mate_copy = start(remote(vg_hbm, pair.at[:, other], vg_send.at[7], vg_recv.at[0], mate))

    def grads_hop(index, src, slot, where):
        return remote(src, grads.at[slot], vg_send.at[index], vg_recv.at[slot], where)

    start(grads_hop(0, flipped, 1, device(1)))
    start(grads_hop(1, flipped, 3, device(3)))
    start(grads_hop(3, flipped, 4, device(4)))

    def pass_grads(slot):
        got_grads(slot)
        if slot == 3:
            start(grads_hop(2, grads.at[3], 2, device(1)))
        start(grads_hop(3 + slot, grads.at[slot], 4 + slot, device(4)))

    swaps = [
        start(remote(
            w.at[weight_rows(b, 1 - c, n, count), :],
            weights.at[b, pl.ds(n * rows_chunk, count * rows_chunk), other],
            w_send.at[index], w_recv.at[index], mate,
        ))
        for index, (b, n, count) in enumerate(weight_pieces)
    ]

    def li_hop(kind, k, src, rows, where):
        return remote(src, parts.at[k, rows, :], li_send.at[kind, k], li_recv.at[kind, k], where)

    direct, shared, to_y, core_direct, core_shared, core_y = ({} for _ in range(6))
    for k in SEND_ORDER:
        if DIRECT:
            direct[k] = li_hop(0, k, li.at[direct_rows, columns(k)], direct_rows, device(k))
            core_direct[k] = li_hop(3, k, parts.at[k, direct_rows, :], direct_rows, mate)
        shared[k] = li_hop(1, k, li.at[my_rows, columns(k)], my_rows, device(k))
        to_y[k] = li_hop(2, k, parts.at[k, my_rows, :], my_rows, across)
        core_shared[k] = li_hop(4, k, parts.at[k, my_rows, :], my_rows, mate)
        core_y[k] = li_hop(5, k, parts.at[k, y_rows, :], y_rows, mate)

    def send_piece(n):
        k = SEND_ORDER[n]
        if DIRECT:
            direct[k].start()
        shared[k].start()

    def sent_piece(n):
        k = SEND_ORDER[n]
        if DIRECT:
            direct[k].wait_send()
        shared[k].wait_send()

    for n in range(WINDOW):
        send_piece(n)

    def product(b, rows):
        return lax.dot_general(
            pair[...], weights[b, rows, :], (((1,), (1,)), ((), ())),
            preferred_element_type=jnp.float32,
        )

    terms = [
        remote(outgoing.at[n], incoming.at[n], term_send.at[n], term_recv.at[n], across)
        for n in range(TERM_CHUNKS)
    ]

    def send_term(n):
        held[n].wait()
        swaps[n].wait_recv()

        @pl.loop(0, rows_chunk // TERM_TILE)
        def _(s):
            at = pl.multiple_of(s * TERM_TILE, TERM_TILE)
            outgoing[n, :, pl.ds(at, TERM_TILE)] = product(
                0, pl.ds(n * rows_chunk + at, TERM_TILE)
            ).astype(jnp.bfloat16)

        start(terms[n])

    def got_grads(slot):
        grads_hop(0, flipped, slot, device(1)).wait_recv()

    def add_partial(k, first):
        side = k // 4

        @pl.loop(0, segment // TILE)
        def _(s):
            at = pl.ds(pl.multiple_of(s * TILE, TILE), TILE)
            value = jnp.dot(
                (flipped if k == 0 else grads.at[k])[...], parts[k, :, at],
                preferred_element_type=jnp.float32,
            )
            value = quantized(value)
            sums[side, :, at] = value if first else sums[side, :, at] + value

    mate_copy.wait_recv()
    for n in range(TERM_CHUNKS):
        send_term(n)
        if n == 1:
            pass_grads(1)
        if n == 3:
            pass_grads(3)

    own_part.wait()
    add_partial(0, True)

    def keep_own_terms():
        held[TERM_CHUNKS].wait()
        swaps[TERM_CHUNKS].wait_recv()

        @pl.loop(0, block // TERM_TILE)
        def _(s):
            at = pl.ds(pl.multiple_of(s * TERM_TILE, TERM_TILE), TERM_TILE)
            own_terms[:, at] = product(1, at)

    def finish_terms():
        for n in range(TERM_CHUNKS):
            terms[n].wait_recv()
            at = pl.ds(n * rows_chunk, rows_chunk)
            ig[:, at] = (own_terms[:, at] + incoming[n].astype(jnp.float32)).astype(jnp.bfloat16)

    started = {0}
    for step in range(len(WAIT_ORDER) + 2):
        if step < len(WAIT_ORDER):
            k = WAIT_ORDER[step]
            if DIRECT:
                direct[k].wait_recv()
                start(core_direct[k])
            shared[k].wait_recv()
            start(to_y[k])
            start(core_shared[k])
            sent_piece(step)
            if step + WINDOW < len(SEND_ORDER):
                send_piece(step + WINDOW)
        if 1 <= step <= len(WAIT_ORDER):
            k = WAIT_ORDER[step - 1]
            to_y[k].wait_recv()
            start(core_y[k])
        if step == 2:
            pass_grads(2)
        if step == 1:
            keep_own_terms()
        if step == len(WAIT_ORDER):
            finish_terms()
        if step >= 2:
            k = WAIT_ORDER[step - 2]
            if DIRECT:
                core_direct[k].wait_recv()
            core_shared[k].wait_recv()
            core_y[k].wait_recv()
            if k >= 4:
                got_grads(k)
            add_partial(k, k // 4 not in started)
            started.add(k // 4)

    @pl.loop(0, segment // TILE)
    def _(s):
        at = pl.ds(pl.multiple_of(s * TILE, TILE), TILE)
        wg[:, at] = (quantized(sums[0, :, at]) + quantized(sums[1, :, at])) * 0.125

    for copy in sent:
        copy.wait_send()


def kernel_body(layer_input, value_grads, value_weight):
    tok, width = layer_input.shape
    cols = value_grads.shape[1]
    segment, block = width // 8, width // 4
    bf16, f32 = jnp.bfloat16, jnp.float32
    dma = pltpu.SemaphoreType.DMA
    in_vmem, in_any = pl.BlockSpec(memory_space=pltpu.VMEM), pl.BlockSpec(memory_space=pltpu.HBM)
    input_grads, weight_grads = pl.pallas_call(
        kernel,
        out_shape=(
            jax.ShapeDtypeStruct((tok, block), bf16),
            jax.ShapeDtypeStruct((cols, segment), f32),
        ),
        in_specs=[in_any, in_any, in_any],
        out_specs=(in_vmem, in_vmem),
        scratch_shapes=[
            pltpu.VMEM((tok, 2 * cols), bf16),
            pltpu.VMEM((cols, tok), bf16),
            pltpu.VMEM((8, tok, segment), bf16),
            pltpu.VMEM((8, cols, tok), bf16),
            pltpu.VMEM((2, block, 2 * cols), bf16),
            pltpu.VMEM((TERM_CHUNKS, tok, block // TERM_CHUNKS), bf16),
            pltpu.VMEM((TERM_CHUNKS, tok, block // TERM_CHUNKS), bf16),
            pltpu.VMEM((tok, block), f32),
            pltpu.VMEM((2, cols, segment), f32),
            dma((6, 8)), dma((6, 8)),
            dma((8,)), dma((8,)),
            dma((TERM_CHUNKS + 1,)), dma((TERM_CHUNKS + 1,)),
            dma((TERM_CHUNKS,)), dma((TERM_CHUNKS,)),
            dma((TERM_CHUNKS + 3,)),
        ],
        compiler_params=pltpu.CompilerParams(
            collective_id=0, has_side_effects=True, vmem_limit_bytes=48 * 1024 * 1024
        ),
        cost_estimate=pl.CostEstimate(
            flops=4 * tok * width * cols, bytes_accessed=12 * 1024 * 1024, transcendentals=0
        ),
    )(layer_input, value_grads, value_weight)
    return input_grads, weight_grads.T


def solution(mesh):
    placed = (P(("inter", "intra"), None), P(("inter", "intra"), "tensor"), P(None, "tensor"))
    sizes = tuple(mesh.shape[name] for name in ("inter", "intra", "tensor"))
    return jax.shard_map(
        kernel_body if sizes == (2, 4, 4) else plain_body,
        mesh=mesh,
        in_specs=placed,
        out_specs=(P(("inter", "intra"), "tensor"), P(("inter", "intra"), "tensor")),
        check_vma=False,
    )
```
